128 devices in a mesh: radial: 32 (over z, y_lo, x), chan: 4 (over y_hi, core).
Axes of the slice: x: 4, y: 4 (y_hi: 2, y_lo: 2; y = y_hi * 2 + y_lo), z: 4, core: 2. Of those that a mesh axis runs over, the one named last changes fastest.
Arguments:
- amplitudes: bfloat16 [256, 2048, 256], P('radial', 'chan'), may hold values from -6 to 6
- previous: bfloat16 [256, 2048, 256], P('radial', 'chan'), may hold values from -6 to 6
- coupling: bfloat16 [256, 2048, 2048], P('radial', 'chan'), may hold values from -0.125 to 0.125
- thresholds: float32 [2048], P('chan'), may hold values from 0 to 2
- barrier: float32 [2048], P('chan'), may hold values from 0.5 to 4
- block_order: int32 [16], replicated, may hold values from 0 to 15, each once
- window_offset: int32 [1], replicated, may hold values from 0 to 7936
Outputs:
- filtered: bfloat16 [256, 2048, 256], P('radial', 'chan')
The draws below stay inside these ranges and needn't reach their ends.
Inputs may be any that keep to these rules, and one draw needn't show every extreme that they name: `block_order`: each of 0 to 15 once.
All inputs are finite; a program needn't handle non-finite values.
Results may differ from the reference program's by a relative error of at most 0.001.
Values may be sent and summed in bfloat16 or wider, within the bound.
A program may use at most 256 MiB of HBM per device.

```python
import math
import jax
import jax.numpy as jnp
from jax import lax

C = 2048
CHB = 128
CBLK = 16
POINTS = 256
GRID = 8192
K = 256


def level_of(rng, extent, split, smallest, top_value):
    def one(axis_at, parts):
        steps = jax.random.uniform(jax.random.fold_in(jax.random.fold_in(rng, 6), axis_at), (parts,), jnp.float32, smallest / len(split), top_value / len(split))
        return jnp.repeat(jnp.exp(steps), extent[axis_at] // parts).reshape((-1,) + (1,) * (len(extent) - axis_at - 1))

    level = one(*split[0])
    for cut in split[1:]:
        level = level * one(*cut)
    return level


def scatter_about(own_key, extent, spread, limit, cuts=(), kind=jnp.bfloat16):
    values = jax.random.normal(own_key, extent, jnp.float32) * spread
    if len(cuts) > 0:
        values = level_of(own_key, extent, cuts, -0.22, 0.18) * values
    return jnp.clip(values, min=-limit, max=limit).astype(kind)


def setup_inputs(seed: int = 0) -> dict:
    splits = jax.random.split(jax.random.key(seed), 8)
    amplitudes = scatter_about(splits[0], (POINTS, C, K), 1.0, 6.0, ((0, 32), (1, 4)))
    previous = scatter_about(splits[1], (POINTS, C, K), 1.0, 6.0, ((0, 32), (1, 4)))
    coupling = scatter_about(splits[2], (POINTS, C, C), C ** -0.5, 0.125, ((0, 32), (1, 4)))
    thresholds = jnp.clip(2.0 * jax.random.uniform(splits[3], (C,), jnp.float32) ** level_of(splits[3], (C,), ((0, 4),), -0.2, 0.2), 0.0, 2.0)
    barrier = jnp.clip(jnp.exp(math.log(4.0) - 2.0794415 * jax.random.uniform(splits[4], (C,), jnp.float32) ** level_of(splits[4], (C,), ((0, 4),), -0.2, 0.2)), 0.5, 4.0)
    block_order = jax.random.permutation(splits[5], CBLK).astype(jnp.int32)
    window_offset = jax.random.randint(splits[6], (1,), 0, GRID - POINTS + 1).astype(jnp.int32)
    return dict(amplitudes=amplitudes, previous=previous, coupling=coupling, thresholds=thresholds, barrier=barrier, block_order=block_order, window_offset=window_offset)


stencil_weights = (-1.0 / 560, 8.0 / 315, -1.0 / 5, 8.0 / 5, -205.0 / 72, 8.0 / 5, -1.0 / 5, 8.0 / 315, -1.0 / 560)


def reference(amplitudes, previous, coupling, thresholds, barrier, block_order, window_offset):
    columns = (block_order[:, None] * CHB + jnp.arange(CHB, dtype=jnp.int32)[None, :]).reshape(-1).astype(jnp.int32)
    ordered = jnp.take(amplitudes, columns, axis=1)

    def one_point(pair):
        matrix, vectors = pair
        return jnp.dot(matrix, vectors, preferred_element_type=jnp.float32)

    potential = lax.map(one_point, (coupling, ordered))
    padded = jnp.pad(amplitudes.astype(jnp.float32), ((4, 4), (0, 0), (0, 0)))
    laplace = jnp.zeros(amplitudes.shape, jnp.float32)
    for shift_index in range(9):
        laplace = laplace + stencil_weights[shift_index] * padded[shift_index:shift_index + POINTS]
    radius = (window_offset[0] + jnp.arange(POINTS, dtype=jnp.int32) + 1).astype(jnp.float32) / (GRID // 16)
    diagonal = thresholds[None, :] + barrier[None, :] / (1.0 + radius[:, None] ** 2)
    applied = -0.5 * laplace + diagonal[:, :, None] * amplitudes.astype(jnp.float32) + potential
    result = 2.0 * (applied - 1.0 * amplitudes.astype(jnp.float32)) / 6.0 - previous.astype(jnp.float32)
    return result.astype(jnp.bfloat16)
```

```python
import functools

import jax
import jax.numpy as jnp
from jax import lax
from jax.experimental import pallas as pl
from jax.experimental.pallas import tpu as pltpu
from jax.sharding import PartitionSpec as P

CHB = 128
GRID = 8192
MESH = pl.DeviceIdType.MESH
TAPS = (-205.0 / 72, 8.0 / 5, -1.0 / 5, 8.0 / 315, -1.0 / 560)
LANES = 128
TILE = 16


def kernel(
    amp, prev, coup, thr, bar, order, offset, out,
    cbuf, vecs, relay_t, relay_a, halo_lo, halo_hi, pbuf, acc, thr_b, bar_b, scale, columns,
    coup_sem, own_sem, prev_sem, out_sem,
    t_send, t_recv, a_send, a_recv, ft_send, fa_send, far_recv,
    sib_send, sib_recv, fs_send, fs_recv, up_send, up_recv, down_send, down_recv,
):
    points, rows, width = amp.shape
    half = points // 2
    per = rows // CHB
    radial, chan = lax.axis_index("radial"), lax.axis_index("chan")
    x, yl, z = radial % 4, (radial // 4) % 2, radial // 8
    yh, core = chan // 2, chan % 2
    last = 3

    def at(px, pyl, pz, pyh, pcore):
        return ((pz * 2 + pyl) * 4 + px, pyh * 2 + pcore)

    toward = at(x, 1 - yl, z, yh, core)
    away = at(x, 1 - yl, z, 1 - yh, core)
    sibling = at(x, yl, z, yh, 1 - core)
    up_z = jnp.where(x == last, z + (1 - yl), z)
    up_to = at((x + 1) % 4, yl, jnp.minimum(up_z, 3), yh, core)
    has_up_to = up_z <= 3
    down_z = jnp.where(x == 0, z - yl, z)
    down_to = at((x + 3) % 4, yl, jnp.maximum(down_z, 0), yh, core)
    has_down_to = down_z >= 0
    up_fz = jnp.where(x == 0, z - (1 - yl), z)
    up_from = at((x + 3) % 4, yl, jnp.maximum(up_fz, 0), yh, core)
    has_up_from = up_fz >= 0
    down_fz = jnp.where(x == last, z + yl, z)
    down_from = at((x + 1) % 4, yl, jnp.minimum(down_fz, 3), yh, core)
    has_down_from = down_fz <= 3
    t_base = jnp.where(x < 2, 0, half)
    a_base = half - t_base

    def remote(src, dst, send, recv, to):
        return pltpu.make_async_remote_copy(
            src_ref=src, dst_ref=dst, send_sem=send, recv_sem=recv, device_id=to, device_id_type=MESH
        )

    def own_t(i):
        return remote(amp.at[t_base + i], relay_t.at[i], t_send.at[i], t_recv.at[i], toward)

    def own_a(i):
        return remote(amp.at[a_base + i], relay_a.at[i], a_send.at[i], a_recv.at[i], away)

    def fwd_t(i):
        p = t_base + i
        return remote(relay_t.at[i], vecs.at[2, p], ft_send.at[i], far_recv.at[p], away)

    def fwd_a(i):
        p = a_base + i
        return remote(relay_a.at[i], vecs.at[2, p], fa_send.at[i], far_recv.at[p], toward)

    def own_sib(p):
        return remote(amp.at[p], vecs.at[1, p], sib_send.at[p], sib_recv.at[p], sibling)

    def fwd_sib(p):
        return remote(vecs.at[2, p], vecs.at[3, p], fs_send.at[p], fs_recv.at[p], sibling)

    def up_own(i):
        return remote(amp.at[half + i], halo_lo.at[i], up_send.at[i], up_recv.at[i], up_to)

    def up_relay(i):
        return remote(relay_t.at[i], halo_lo.at[i], up_send.at[i], up_recv.at[i], up_to)

    def down_own(i):
        return remote(amp.at[i], halo_hi.at[i], down_send.at[i], down_recv.at[i], down_to)

    def down_relay(i):
        return remote(relay_t.at[i], halo_hi.at[i], down_send.at[i], down_recv.at[i], down_to)

    blocks = coup.shape[2] // CHB

    def coup_copy(p, b):
        part = coup.at[p, :, b * CHB : (b + 1) * CHB]
        return pltpu.make_async_copy(part, cbuf.at[p, b], coup_sem.at[p, b])

    def coup_all(step):
        def one(p, _):
            for b in range(blocks):
                step(coup_copy(p, b))
            return 0

        lax.fori_loop(0, points, one, 0)

    own_copy = pltpu.make_async_copy(amp, vecs.at[0], own_sem)
    prev_copy = pltpu.make_async_copy(prev, pbuf, prev_sem)

    def out_copy(p):
        return pltpu.make_async_copy(pbuf.at[p], out.at[p], out_sem.at[p])

    barrier = pltpu.get_barrier_semaphore()
    for to in (toward, away, sibling):
        pl.semaphore_signal(barrier, inc=1, device_id=to, device_id_type=MESH)

    @pl.when(has_up_from)
    def _():
        pl.semaphore_signal(barrier, inc=1, device_id=up_from, device_id_type=MESH)

    @pl.when(has_down_from)
    def _():
        pl.semaphore_signal(barrier, inc=1, device_id=down_from, device_id_type=MESH)

    own_copy.start()
    pl.semaphore_wait(
        barrier, 3 + jnp.where(has_up_to, 1, 0) + jnp.where(has_down_to, 1, 0)
    )
    for i in range(half):
        own_t(i).start()
        own_a(i).start()
    for p in range(points):
        own_sib(p).start()
    for i in range(half):
        @pl.when(x < last)
        def _(i=i):
            up_own(i).start()

        @pl.when(x > 0)
        def _(i=i):
            down_own(i).start()
    coup_all(lambda c: c.start())
    prev_copy.start()

    @pl.when(jnp.logical_not(has_up_from))
    def _():
        halo_lo[...] = jnp.zeros_like(halo_lo)

    @pl.when(jnp.logical_not(has_down_from))
    def _():
        halo_hi[...] = jnp.zeros_like(halo_hi)

    for j in range(per):
        part = slice(j * CHB, (j + 1) * CHB)
        thr_b[part, :] = jnp.broadcast_to(thr[part].reshape(1, CHB), (CHB, LANES)).T
        bar_b[part, :] = jnp.broadcast_to(bar[part].reshape(1, CHB), (CHB, LANES)).T
    for p in range(points):
        place = jnp.full((TILE, LANES), offset[0] + radial * points + p + 1, jnp.int32)
        s = place.astype(jnp.float32) * (1.0 / (GRID // 16))
        scale[p] = 1.0 / (1.0 + s * s)

    own_copy.wait()
    coup_all(lambda c: c.wait())

    sources = (chan, yh * 2 + 1 - core, (1 - yh) * 2 + core, (1 - yh) * 2 + 1 - core)

    def column(j):
        found = jnp.int32(0)
        for b in range(order.shape[0]):
            found = found + b * (1 - jnp.minimum((order[b] - j) * (order[b] - j), 1))
        return jnp.minimum(found, order.shape[0] - 1)

    for k, s in enumerate(sources):
        for j in range(per):
            columns[k * per + j] = column(s * per + j)

    def product(p, which):
        lhs = jnp.concatenate(
            [
                cbuf[p, columns[s * per + j]]
                for s in which
                for j in range(per)
            ],
            axis=1,
        )
        rhs = jnp.concatenate([vecs[s, p] for s in which], axis=0)
        return jnp.dot(lhs, rhs, preferred_element_type=jnp.float32)

    def first_hop(i, _):
        t = own_t(i)
        t.wait_recv()
        fwd_t(i).start()

        @pl.when(jnp.logical_and(x == last, has_up_to))
        def _():
            up_relay(i).start()

        @pl.when(jnp.logical_and(x == 0, has_down_to))
        def _():
            down_relay(i).start()

        own_a(i).wait_recv()
        fwd_a(i).start()

        def local(q, _):
            p = i * 2 + q
            own_sib(p).wait_recv()
            acc[p] = product(p, (0, 1))
            return 0

        lax.fori_loop(0, 2, local, 0)
        return 0

    lax.fori_loop(0, half, first_hop, 0)

    def arrive(i):
        for p in (t_base + i, a_base + i):
            remote(vecs.at[2, p], vecs.at[2, p], ft_send.at[i], far_recv.at[p], away).wait_recv()
            fwd_sib(p).start()

    def finish(i, write):
        def one(q, _):
            p = i + q * half
            fwd_sib(p).wait_recv()
            if write:
                pbuf[p] = ((acc[p] + product(p, (2, 3))) * (1.0 / 3.0)).astype(pbuf.dtype)
                out_copy(p).start()
            else:
                acc[p] += product(p, (2, 3))
            return 0

        lax.fori_loop(0, 2, one, 0)

    def store(i):
        for p in (i, i + half):
            pbuf[p] = (acc[p] * (1.0 / 3.0)).astype(pbuf.dtype)
            out_copy(p).start()

    arrive(0)
    finish(0, False)
    arrive(1)
    finish(1, False)

    @pl.when(has_up_from)
    def _():
        for i in range(half):
            up_own(i).wait_recv()

    @pl.when(has_down_from)
    def _():
        for i in range(half):
            down_own(i).wait_recv()

    prev_copy.wait()

    def stencil(r, _):
        tile = pl.ds(pl.multiple_of(r * TILE, TILE), TILE)
        for l in range(width // LANES):
            lane = slice(l * LANES, (l + 1) * LANES)
            v = [halo_lo[i, tile, lane].astype(jnp.float32) for i in range(half)]
            v += [vecs[0, i, tile, lane].astype(jnp.float32) for i in range(points)]
            v += [halo_hi[i, tile, lane].astype(jnp.float32) for i in range(half)]
            base = thr_b[tile, :] - (1.0 + 0.5 * TAPS[0])
            slope = bar_b[tile, :]
            for p in range(points):
                c = p + half
                total = (base + slope * scale[p]) * v[c]
                for m in range(1, 5):
                    total = total + (-0.5 * TAPS[m]) * (v[c - m] + v[c + m])
                total = total - 3.0 * pbuf[p, tile, lane].astype(jnp.float32)
                acc[p, tile, lane] = acc[p, tile, lane] + total
        return 0

    lax.fori_loop(0, rows // TILE, stencil, 0)
    store(0)
    store(1)
    arrive(2)
    finish(2, True)
    arrive(3)
    finish(3, True)

    for i in range(half):
        own_t(i).wait_send()
        own_a(i).wait_send()
        fwd_t(i).wait_send()
        fwd_a(i).wait_send()
    for p in range(points):
        own_sib(p).wait_send()
        fwd_sib(p).wait_send()

    @pl.when(has_up_to)
    def _():
        for i in range(half):
            up_relay(i).wait_send()

    @pl.when(has_down_to)
    def _():
        for i in range(half):
            down_relay(i).wait_send()

    for p in range(points):
        out_copy(p).wait()


def local(amplitudes, previous, coupling, thresholds, barrier, block_order, window_offset):
    points, rows, width = amplitudes.shape
    half = points // 2
    columns = coupling.shape[2]
    bf16, f32 = jnp.bfloat16, jnp.float32
    sem = pltpu.SemaphoreType.DMA
    any_spec = pl.BlockSpec(memory_space=pl.ANY)
    vmem_spec = pl.BlockSpec(memory_space=pltpu.VMEM)
    smem_spec = pl.BlockSpec(memory_space=pltpu.SMEM)
    return pl.pallas_call(
        kernel,
        out_shape=jax.ShapeDtypeStruct((points, rows, width), bf16),
        in_specs=[any_spec] * 3 + [vmem_spec] * 2 + [smem_spec] * 2,
        out_specs=any_spec,
        scratch_shapes=[
            pltpu.VMEM((points, columns // CHB, rows, CHB), bf16),
            pltpu.VMEM((4, points, rows, width), bf16),
            pltpu.VMEM((half, rows, width), bf16),
            pltpu.VMEM((half, rows, width), bf16),
            pltpu.VMEM((half, rows, width), bf16),
            pltpu.VMEM((half, rows, width), bf16),
            pltpu.VMEM((points, rows, width), bf16),
            pltpu.VMEM((points, rows, width), f32),
            pltpu.VMEM((rows, LANES), f32),
            pltpu.VMEM((rows, LANES), f32),
            pltpu.VMEM((points, TILE, LANES), f32),
            pltpu.SMEM((columns // CHB,), jnp.int32),
            sem((points, columns // CHB)), sem, sem, sem((points,)),
            sem((half,)), sem((half,)), sem((half,)), sem((half,)),
            sem((half,)), sem((half,)), sem((points,)),
            sem((points,)), sem((points,)), sem((points,)), sem((points,)),
            sem((half,)), sem((half,)), sem((half,)), sem((half,)),
        ],
        compiler_params=pltpu.CompilerParams(
            collective_id=0, has_side_effects=True, vmem_limit_bytes=60 << 20
        ),
        cost_estimate=pl.CostEstimate(
            flops=2 * points * rows * columns * width,
            bytes_accessed=2 * points * rows * (columns + 3 * width),
            transcendentals=0,
        ),
    )(amplitudes, previous, coupling, thresholds, barrier, block_order, window_offset)


def solution(mesh):
    placed = (
        P("radial", "chan", None),
        P("radial", "chan", None),
        P("radial", "chan", None),
        P("chan"),
        P("chan"),
        P(),
        P(),
    )
    return jax.shard_map(
        local, mesh=mesh, in_specs=placed, out_specs=P("radial", "chan", None), check_vma=False
    )
```

```python
import functools

import jax
import jax.numpy as jnp
from jax import lax
from jax.experimental import pallas as pl
from jax.experimental.pallas import tpu as pltpu
from jax.sharding import PartitionSpec as P

CHB = 128
GRID = 8192
MESH = pl.DeviceIdType.MESH
TAPS = (-205.0 / 72, 8.0 / 5, -1.0 / 5, 8.0 / 315, -1.0 / 560)
LANES = 128
TILE = 16


def kernel(
    amp, prev, coup, thr_in, bar_in, order_in, offset_in, out,
    cbuf, vecs, relay_t, relay_a, halo_lo, halo_hi, pbuf, acc, thr_b, bar_b, scale, columns,
    thr, bar, order, offset, small_sem,
    coup_sem, own_sem, prev_sem,
    t_send, t_recv, a_send, a_recv, ft_send, fa_send, far_recv,
    sib_send, sib_recv, fs_send, fs_recv, up_send, up_recv, down_send, down_recv,
):
    points, rows, width = amp.shape
    half = points // 2
    per = rows // CHB
    radial, chan = lax.axis_index("radial"), lax.axis_index("chan")
    x, yl, z = radial % 4, (radial // 4) % 2, radial // 8
    yh, core = chan // 2, chan % 2
    last = 3

    def at(px, pyl, pz, pyh, pcore):
        return ((pz * 2 + pyl) * 4 + px, pyh * 2 + pcore)

    toward = at(x, 1 - yl, z, yh, core)
    away = at(x, 1 - yl, z, 1 - yh, core)
    sibling = at(x, yl, z, yh, 1 - core)
    up_z = jnp.where(x == last, z + (1 - yl), z)
    up_to = at((x + 1) % 4, yl, jnp.minimum(up_z, 3), yh, core)
    has_up_to = up_z <= 3
    down_z = jnp.where(x == 0, z - yl, z)
    down_to = at((x + 3) % 4, yl, jnp.maximum(down_z, 0), yh, core)
    has_down_to = down_z >= 0
    up_fz = jnp.where(x == 0, z - (1 - yl), z)
    up_from = at((x + 3) % 4, yl, jnp.maximum(up_fz, 0), yh, core)
    has_up_from = up_fz >= 0
    down_fz = jnp.where(x == last, z + yl, z)
    down_from = at((x + 1) % 4, yl, jnp.minimum(down_fz, 3), yh, core)
    has_down_from = down_fz <= 3
    t_base = jnp.where(x < 2, 0, half)
    a_base = half - t_base

    def remote(src, dst, send, recv, to):
        return pltpu.make_async_remote_copy(
            src_ref=src, dst_ref=dst, send_sem=send, recv_sem=recv, device_id=to, device_id_type=MESH
        )

    def own_t(i):
        return remote(amp.at[t_base + i], relay_t.at[i], t_send.at[i], t_recv.at[i], toward)

    def own_a(i):
        return remote(amp.at[a_base + i], relay_a.at[i], a_send.at[i], a_recv.at[i], away)

    def fwd_t(i):
        p = t_base + i
        return remote(relay_t.at[i], vecs.at[2, p], ft_send.at[i], far_recv.at[p], away)

    def fwd_a(i):
        p = a_base + i
        return remote(relay_a.at[i], vecs.at[2, p], fa_send.at[i], far_recv.at[p], toward)

    def own_sib(p):
        return remote(amp.at[p], vecs.at[1, p], sib_send.at[p], sib_recv.at[p], sibling)

    def fwd_sib(p):
        return remote(vecs.at[2, p], vecs.at[3, p], fs_send.at[p], fs_recv.at[p], sibling)

    def up_own(i):
        return remote(amp.at[half + i], halo_lo.at[i], up_send.at[i], up_recv.at[i], up_to)

    def up_relay(i):
        return remote(relay_t.at[i], halo_lo.at[i], up_send.at[i], up_recv.at[i], up_to)

    def down_own(i):
        return remote(amp.at[i], halo_hi.at[i], down_send.at[i], down_recv.at[i], down_to)

    def down_relay(i):
        return remote(relay_t.at[i], halo_hi.at[i], down_send.at[i], down_recv.at[i], down_to)

    blocks = coup.shape[2] // CHB

    def coup_copy(p, b):
        part = coup.at[p, :, b * CHB : (b + 1) * CHB]
        return pltpu.make_async_copy(part, cbuf.at[p, b], coup_sem.at[p, b])

    def coup_all(step):
        def one(p, _):
            for b in range(blocks):
                step(coup_copy(p, b))
            return 0

        lax.fori_loop(0, points, one, 0)

    small = [
        pltpu.make_async_copy(a, b, small_sem.at[i])
        for i, (a, b) in enumerate(
            ((thr_in, thr), (bar_in, bar), (order_in, order), (offset_in, offset))
        )
    ]
    own_copy = pltpu.make_async_copy(amp, vecs.at[0], own_sem)
    prev_copy = pltpu.make_async_copy(prev, pbuf, prev_sem)

    barrier = pltpu.get_barrier_semaphore()
    for to in (toward, away, sibling):
        pl.semaphore_signal(barrier, inc=1, device_id=to, device_id_type=MESH)

    @pl.when(has_up_from)
    def _():
        pl.semaphore_signal(barrier, inc=1, device_id=up_from, device_id_type=MESH)

    @pl.when(has_down_from)
    def _():
        pl.semaphore_signal(barrier, inc=1, device_id=down_from, device_id_type=MESH)

    own_copy.start()
    for copy in small:
        copy.start()
    pl.semaphore_wait(
        barrier, 3 + jnp.where(has_up_to, 1, 0) + jnp.where(has_down_to, 1, 0)
    )
    for i in range(half):
        own_t(i).start()
        own_a(i).start()
    for p in range(points):
        own_sib(p).start()
    for i in range(half):
        @pl.when(x < last)
        def _(i=i):
            up_own(i).start()

        @pl.when(x > 0)
        def _(i=i):
            down_own(i).start()
    coup_all(lambda c: c.start())
    prev_copy.start()

    @pl.when(jnp.logical_not(has_up_from))
    def _():
        halo_lo[...] = jnp.zeros_like(halo_lo)

    @pl.when(jnp.logical_not(has_down_from))
    def _():
        halo_hi[...] = jnp.zeros_like(halo_hi)

    for copy in small:
        copy.wait()
    for j in range(per):
        part = slice(j * CHB, (j + 1) * CHB)
        thr_b[part, :] = jnp.broadcast_to(thr[part].reshape(1, CHB), (CHB, LANES)).T
        bar_b[part, :] = jnp.broadcast_to(bar[part].reshape(1, CHB), (CHB, LANES)).T
    for p in range(points):
        place = jnp.full((TILE, LANES), offset[0] + radial * points + p + 1, jnp.int32)
        s = place.astype(jnp.float32) * (1.0 / (GRID // 16))
        scale[p] = 1.0 / (1.0 + s * s)

    own_copy.wait()
    coup_all(lambda c: c.wait())

    sources = (chan, yh * 2 + 1 - core, (1 - yh) * 2 + core, (1 - yh) * 2 + 1 - core)

    def column(j):
        found = jnp.int32(0)
        for b in range(order.shape[0]):
            found = found + b * (1 - jnp.minimum((order[b] - j) * (order[b] - j), 1))
        return jnp.minimum(found, order.shape[0] - 1)

    for k, s in enumerate(sources):
        for j in range(per):
            columns[k * per + j] = column(s * per + j)

    def product(p, which):
        lhs = jnp.concatenate(
            [
                cbuf[p, columns[s * per + j]]
                for s in which
                for j in range(per)
            ],
            axis=1,
        )
        rhs = jnp.concatenate([vecs[s, p] for s in which], axis=0)
        return jnp.dot(lhs, rhs, preferred_element_type=jnp.float32)

    def first_hop(i, _):
        t = own_t(i)
        t.wait_recv()
        fwd_t(i).start()

        @pl.when(jnp.logical_and(x == last, has_up_to))
        def _():
            up_relay(i).start()

        @pl.when(jnp.logical_and(x == 0, has_down_to))
        def _():
            down_relay(i).start()

        own_a(i).wait_recv()
        fwd_a(i).start()

        def local(q, _):
            p = i * 2 + q
            own_sib(p).wait_recv()
            acc[p] = product(p, (0, 1))
            return 0

        lax.fori_loop(0, 2, local, 0)
        return 0

    lax.fori_loop(0, half, first_hop, 0)

    def arrive(i):
        for p in (t_base + i, a_base + i):
            remote(vecs.at[2, p], vecs.at[2, p], ft_send.at[i], far_recv.at[p], away).wait_recv()
            fwd_sib(p).start()

    def finish(i, write):
        def one(q, _):
            p = i + q * half
            fwd_sib(p).wait_recv()
            if write:
                out[p] = ((acc[p] + product(p, (2, 3))) * (1.0 / 3.0)).astype(out.dtype)
            else:
                acc[p] += product(p, (2, 3))
            return 0

        lax.fori_loop(0, 2, one, 0)

    def store(i):
        for p in (i, i + half):
            out[p] = (acc[p] * (1.0 / 3.0)).astype(out.dtype)

    arrive(0)
    finish(0, False)
    arrive(1)
    finish(1, False)

    @pl.when(has_up_from)
    def _():
        for i in range(half):
            up_own(i).wait_recv()

    @pl.when(has_down_from)
    def _():
        for i in range(half):
            down_own(i).wait_recv()

    prev_copy.wait()

    def stencil(r, _):
        tile = pl.ds(pl.multiple_of(r * TILE, TILE), TILE)
        for l in range(width // LANES):
            lane = slice(l * LANES, (l + 1) * LANES)
            v = [halo_lo[i, tile, lane].astype(jnp.float32) for i in range(half)]
            v += [vecs[0, i, tile, lane].astype(jnp.float32) for i in range(points)]
            v += [halo_hi[i, tile, lane].astype(jnp.float32) for i in range(half)]
            base = thr_b[tile, :] - (1.0 + 0.5 * TAPS[0])
            slope = bar_b[tile, :]
            for p in range(points):
                c = p + half
                total = (base + slope * scale[p]) * v[c]
                for m in range(1, 5):
                    total = total + (-0.5 * TAPS[m]) * (v[c - m] + v[c + m])
                total = total - 3.0 * pbuf[p, tile, lane].astype(jnp.float32)
                acc[p, tile, lane] = acc[p, tile, lane] + total
        return 0

    lax.fori_loop(0, rows // TILE, stencil, 0)
    store(0)
    store(1)
    arrive(2)
    finish(2, True)
    arrive(3)
    finish(3, True)

    for i in range(half):
        own_t(i).wait_send()
        own_a(i).wait_send()
        fwd_t(i).wait_send()
        fwd_a(i).wait_send()
    for p in range(points):
        own_sib(p).wait_send()
        fwd_sib(p).wait_send()

    @pl.when(has_up_to)
    def _():
        for i in range(half):
            up_relay(i).wait_send()

    @pl.when(has_down_to)
    def _():
        for i in range(half):
            down_relay(i).wait_send()


def write_out(staged, out, sems):
    copies = [
        pltpu.make_async_copy(staged.at[p], out.at[p], sems.at[p])
        for p in range(staged.shape[0])
    ]
    for copy in copies:
        copy.start()
    for copy in copies:
        copy.wait()


def local(amplitudes, previous, coupling, thresholds, barrier, block_order, window_offset):
    points, rows, width = amplitudes.shape
    half = points // 2
    columns = coupling.shape[2]
    bf16, f32 = jnp.bfloat16, jnp.float32
    sem = pltpu.SemaphoreType.DMA
    any_spec = pl.BlockSpec(memory_space=pl.ANY)
    vmem_spec = pl.BlockSpec(memory_space=pltpu.VMEM)
    staged = pl.pallas_call(
        kernel,
        out_shape=pltpu.VMEM((points, rows, width), bf16),
        in_specs=[any_spec] * 7,
        out_specs=vmem_spec,
        scratch_shapes=[
            pltpu.VMEM((points, columns // CHB, rows, CHB), bf16),
            pltpu.VMEM((4, points, rows, width), bf16),
            pltpu.VMEM((half, rows, width), bf16),
            pltpu.VMEM((half, rows, width), bf16),
            pltpu.VMEM((half, rows, width), bf16),
            pltpu.VMEM((half, rows, width), bf16),
            pltpu.VMEM((points, rows, width), bf16),
            pltpu.VMEM((points, rows, width), f32),
            pltpu.VMEM((rows, LANES), f32),
            pltpu.VMEM((rows, LANES), f32),
            pltpu.VMEM((points, TILE, LANES), f32),
            pltpu.SMEM((columns // CHB,), jnp.int32),
            pltpu.VMEM(thresholds.shape, f32),
            pltpu.VMEM(barrier.shape, f32),
            pltpu.SMEM(block_order.shape, jnp.int32),
            pltpu.SMEM(window_offset.shape, jnp.int32),
            sem((4,)),
            sem((points, columns // CHB)), sem, sem,
            sem((half,)), sem((half,)), sem((half,)), sem((half,)),
            sem((half,)), sem((half,)), sem((points,)),
            sem((points,)), sem((points,)), sem((points,)), sem((points,)),
            sem((half,)), sem((half,)), sem((half,)), sem((half,)),
        ],
        compiler_params=pltpu.CompilerParams(
            collective_id=0, has_side_effects=True, vmem_limit_bytes=60 << 20
        ),
        cost_estimate=pl.CostEstimate(
            flops=2 * points * rows * columns * width,
            bytes_accessed=2 * points * rows * (columns + 3 * width),
            transcendentals=0,
        ),
    )(amplitudes, previous, coupling, thresholds, barrier, block_order, window_offset)
    return pl.pallas_call(
        write_out,
        out_shape=jax.ShapeDtypeStruct((points, rows, width), bf16),
        in_specs=[vmem_spec],
        out_specs=any_spec,
        scratch_shapes=[sem((points,))],
        compiler_params=pltpu.CompilerParams(vmem_limit_bytes=40 << 20),
    )(staged)


def solution(mesh):
    placed = (
        P("radial", "chan", None),
        P("radial", "chan", None),
        P("radial", "chan", None),
        P("chan"),
        P("chan"),
        P(),
        P(),
    )
    return jax.shard_map(
        local, mesh=mesh, in_specs=placed, out_specs=P("radial", "chan", None), check_vma=False
    )
```

```python
import functools

import jax
import jax.numpy as jnp
from jax import lax
from jax.experimental import pallas as pl
from jax.experimental.pallas import tpu as pltpu
from jax.sharding import PartitionSpec as P

CHB = 128
GRID = 8192
SPLIT = 2
MESH = pl.DeviceIdType.MESH
TAPS = (-205.0 / 72, 8.0 / 5, -1.0 / 5, 8.0 / 315, -1.0 / 560)
LANES = 128
TILE = 16


def kernel(
    amp, prev, coup, thr_in, bar_in, order_in, offset_in, out,
    cbuf, vecs, relay_t, relay_a, halo_lo, halo_hi, pbuf, acc, thr_b, bar_b, scale, columns,
    thr, bar, order, offset, small_sem,
    coup_sem, own_sem, prev_sem,
    t_send, t_recv, a_send, a_recv, ft_send, fa_send, far_recv,
    sib_send, sib_recv, fs_send, fs_recv, up_send, up_recv, down_send, down_recv,
):
    points, rows, width = amp.shape
    half = points // 2
    per = rows // CHB
    radial, chan = lax.axis_index("radial"), lax.axis_index("chan")
    x, yl, z = radial % 4, (radial // 4) % 2, radial // 8
    yh, core = chan // 2, chan % 2
    last = 3
    pieces = half * SPLIT
    size = rows // SPLIT
    far = vecs.at[2]

    def at(px, pyl, pz, pyh, pcore):
        return ((pz * 2 + pyl) * 4 + px, pyh * 2 + pcore)

    toward = at(x, 1 - yl, z, yh, core)
    away = at(x, 1 - yl, z, 1 - yh, core)
    sibling = at(x, yl, z, yh, 1 - core)
    up_z = jnp.where(x == last, z + (1 - yl), z)
    up_to = at((x + 1) % 4, yl, jnp.minimum(up_z, 3), yh, core)
    has_up_to = up_z <= 3
    down_z = jnp.where(x == 0, z - yl, z)
    down_to = at((x + 3) % 4, yl, jnp.maximum(down_z, 0), yh, core)
    has_down_to = down_z >= 0
    up_fz = jnp.where(x == 0, z - (1 - yl), z)
    up_from = at((x + 3) % 4, yl, jnp.maximum(up_fz, 0), yh, core)
    has_up_from = up_fz >= 0
    down_fz = jnp.where(x == last, z + yl, z)
    down_from = at((x + 1) % 4, yl, jnp.minimum(down_fz, 3), yh, core)
    has_down_from = down_fz <= 3
    t_base = jnp.where(x < 2, 0, half)
    a_base = half - t_base

    def remote(src, dst, send, recv, to):
        return pltpu.make_async_remote_copy(
            src_ref=src, dst_ref=dst, send_sem=send, recv_sem=recv, device_id=to, device_id_type=MESH
        )

    def piece(ref, first, i):
        row = pl.multiple_of((i % SPLIT) * size, size)
        return ref.at[first + i // SPLIT, pl.ds(row, size)]

    def own_t(i):
        return remote(
            piece(amp, t_base, i), piece(relay_t, 0, i), t_send, t_recv.at[i], toward
        )

    def own_a(i):
        return remote(
            piece(amp, a_base, i), piece(relay_a, 0, i), a_send, a_recv.at[i], away
        )

    def fwd_t(i):
        landed = far_recv.at[t_base * SPLIT + i]
        return remote(piece(relay_t, 0, i), piece(far, t_base, i), ft_send, landed, away)

    def fwd_a(i):
        landed = far_recv.at[a_base * SPLIT + i]
        return remote(piece(relay_a, 0, i), piece(far, a_base, i), fa_send, landed, toward)

    def own_sib(p):
        return remote(amp.at[p], vecs.at[1, p], sib_send, sib_recv.at[p], sibling)

    def fwd_sib(q):
        return remote(
            piece(far, 0, q), piece(vecs.at[3], 0, q), fs_send, fs_recv.at[q], sibling
        )

    def up_own(i):
        return remote(amp.at[half + i], halo_lo.at[i], up_send, up_recv, up_to)

    def up_relay(i):
        return remote(relay_t.at[i], halo_lo.at[i], up_send, up_recv, up_to)

    def down_own(i):
        return remote(amp.at[i], halo_hi.at[i], down_send, down_recv, down_to)

    def down_relay(i):
        return remote(relay_t.at[i], halo_hi.at[i], down_send, down_recv, down_to)

    blocks = coup.shape[2] // CHB

    def coup_copy(p, b):
        part = coup.at[p, :, b * CHB : (b + 1) * CHB]
        return pltpu.make_async_copy(part, cbuf.at[p, b], coup_sem.at[p, b])

    def coup_all(step):
        def one(p, _):
            for b in range(blocks):
                step(coup_copy(p, b))
            return 0

        lax.fori_loop(0, points, one, 0)

    small = [
        pltpu.make_async_copy(a, b, small_sem.at[i])
        for i, (a, b) in enumerate(
            ((thr_in, thr), (bar_in, bar), (order_in, order), (offset_in, offset))
        )
    ]
    own_copy = pltpu.make_async_copy(amp, vecs.at[0], own_sem)
    prev_copy = pltpu.make_async_copy(prev, pbuf, prev_sem)

    barrier = pltpu.get_barrier_semaphore()
    for to in (toward, away, sibling):
        pl.semaphore_signal(barrier, inc=1, device_id=to, device_id_type=MESH)

    @pl.when(has_up_from)
    def _():
        pl.semaphore_signal(barrier, inc=1, device_id=up_from, device_id_type=MESH)

    @pl.when(has_down_from)
    def _():
        pl.semaphore_signal(barrier, inc=1, device_id=down_from, device_id_type=MESH)

    own_copy.start()
    for copy in small:
        copy.start()
    pl.semaphore_wait(
        barrier, 3 + jnp.where(has_up_to, 1, 0) + jnp.where(has_down_to, 1, 0)
    )

    def send_own(i, _):
        own_t(i).start()
        own_a(i).start()
        return 0

    for i in range(pieces):
        send_own(i, 0)
    for p in range(points):
        own_sib(p).start()
    for i in range(half):
        @pl.when(x < last)
        def _(i=i):
            up_own(i).start()

        @pl.when(x > 0)
        def _(i=i):
            down_own(i).start()
    coup_all(lambda c: c.start())
    prev_copy.start()

    @pl.when(jnp.logical_not(has_up_from))
    def _():
        halo_lo[...] = jnp.zeros_like(halo_lo)

    @pl.when(jnp.logical_not(has_down_from))
    def _():
        halo_hi[...] = jnp.zeros_like(halo_hi)

    for copy in small:
        copy.wait()
    for j in range(per):
        part = slice(j * CHB, (j + 1) * CHB)
        thr_b[part, :] = jnp.broadcast_to(thr[part].reshape(1, CHB), (CHB, LANES)).T
        bar_b[part, :] = jnp.broadcast_to(bar[part].reshape(1, CHB), (CHB, LANES)).T
    for p in range(points):
        place = jnp.full((TILE, LANES), offset[0] + radial * points + p + 1, jnp.int32)
        s = place.astype(jnp.float32) * (1.0 / (GRID // 16))
        scale[p] = 1.0 / (1.0 + s * s)

    own_copy.wait()
    coup_all(lambda c: c.wait())

    sources = (chan, yh * 2 + 1 - core, (1 - yh) * 2 + core, (1 - yh) * 2 + 1 - core)

    def column(j):
        found = jnp.int32(0)
        for b in range(order.shape[0]):
            found = found + b * (1 - jnp.minimum((order[b] - j) * (order[b] - j), 1))
        return jnp.minimum(found, order.shape[0] - 1)

    for k, s in enumerate(sources):
        for j in range(per):
            columns[k * per + j] = column(s * per + j)

    def product(p, which, first=0, end=per):
        lhs = jnp.concatenate(
            [cbuf[p, columns[s * per + j]] for s in which for j in range(first, end)], axis=1
        )
        part = slice(first * CHB, end * CHB)
        rhs = jnp.concatenate([vecs[s, p, part, :] for s in which], axis=0)
        return jnp.dot(lhs, rhs, preferred_element_type=jnp.float32)

    def near_product(p, _):
        own_sib(p).wait_recv()
        acc[p] = product(p, (0, 1))
        return 0

    def first_hop(g, _):
        def pass_on(j, _):
            i = g * SPLIT + j
            own_t(i).wait_recv()
            fwd_t(i).start()
            own_a(i).wait_recv()
            fwd_a(i).start()
            return 0

        lax.fori_loop(0, SPLIT, pass_on, 0)

        @pl.when(jnp.logical_and(x == last, has_up_to))
        def _():
            up_relay(g).start()

        @pl.when(jnp.logical_and(x == 0, has_down_to))
        def _():
            down_relay(g).start()

        return 0

    lax.fori_loop(0, points, near_product, 0)
    lax.fori_loop(0, half, first_hop, 0)

    def arrive(i):
        def one(j, _):
            for base in (t_base, a_base):
                q = (base + i) * SPLIT + j
                here = piece(far, 0, q)
                remote(here, here, ft_send, far_recv.at[q], away).wait_recv()
                fwd_sib(q).start()
            return 0

        lax.fori_loop(0, SPLIT, one, 0)

    def passed(p, first, end):
        for j in range(first, end):
            fwd_sib(p * SPLIT + j).wait_recv()

    def finish(i):
        def one(h, _):
            p = i + h * half
            passed(p, 0, SPLIT)
            acc[p] += product(p, (2, 3))
            return 0

        lax.fori_loop(0, 2, one, 0)

    def finish_last(i):
        early = per - per // SPLIT

        def far_part(h, _):
            p = i + h * half
            acc[p] += product(p, (2,))
            return 0

        def near_part(h, _):
            p = i + h * half
            passed(p, 0, SPLIT - 1)
            acc[p] += product(p, (3,), 0, early)
            return 0

        def end_part(h, _):
            p = i + h * half
            passed(p, SPLIT - 1, SPLIT)
            total = acc[p] + product(p, (3,), early, per)
            out[p] = (total * (1.0 / 3.0)).astype(out.dtype)
            return 0

        lax.fori_loop(0, 2, far_part, 0)
        far_half = far.at[pl.ds(0, half)]
        remote(relay_t, far_half, ft_send, far_recv.at[0], away).wait_send()
        remote(relay_a, far_half, fa_send, far_recv.at[0], toward).wait_send()
        lax.fori_loop(0, 2, near_part, 0)
        lax.fori_loop(0, 2, end_part, 0)

    def store(i):
        for p in (i, i + half):
            out[p] = (acc[p] * (1.0 / 3.0)).astype(out.dtype)

    arrive(0)
    finish(0)
    arrive(1)
    finish(1)

    first_half = amp.at[pl.ds(0, half)]

    @pl.when(has_up_from)
    def _():
        remote(first_half, halo_lo, up_send, up_recv, up_to).wait_recv()

    @pl.when(has_down_from)
    def _():
        remote(first_half, halo_hi, down_send, down_recv, down_to).wait_recv()

    remote(amp, vecs.at[1], sib_send, sib_recv.at[0], sibling).wait_send()
    remote(first_half, relay_t, t_send, t_recv.at[0], toward).wait_send()
    remote(first_half, relay_a, a_send, a_recv.at[0], away).wait_send()

    @pl.when(has_up_to)
    def _():
        remote(first_half, halo_lo, up_send, up_recv, up_to).wait_send()

    @pl.when(has_down_to)
    def _():
        remote(first_half, halo_hi, down_send, down_recv, down_to).wait_send()

    prev_copy.wait()

    def stencil(r, _):
        tile = pl.ds(pl.multiple_of(r * TILE, TILE), TILE)
        for l in range(width // LANES):
            lane = slice(l * LANES, (l + 1) * LANES)
            v = [halo_lo[i, tile, lane].astype(jnp.float32) for i in range(half)]
            v += [vecs[0, i, tile, lane].astype(jnp.float32) for i in range(points)]
            v += [halo_hi[i, tile, lane].astype(jnp.float32) for i in range(half)]
            base = thr_b[tile, :] - (1.0 + 0.5 * TAPS[0])
            slope = bar_b[tile, :]
            for p in range(points):
                c = p + half
                total = (base + slope * scale[p]) * v[c]
                for m in range(1, 5):
                    total = total + (-0.5 * TAPS[m]) * (v[c - m] + v[c + m])
                total = total - 3.0 * pbuf[p, tile, lane].astype(jnp.float32)
                acc[p, tile, lane] = acc[p, tile, lane] + total
        return 0

    lax.fori_loop(0, rows // TILE, stencil, 0)
    store(0)
    store(1)
    arrive(2)
    finish(2)
    store(2)
    arrive(3)
    finish_last(3)

    remote(far, vecs.at[3], fs_send, fs_recv.at[0], sibling).wait_send()


def write_out(staged, out, sems):
    copies = [
        pltpu.make_async_copy(staged.at[p], out.at[p], sems.at[p])
        for p in range(staged.shape[0])
    ]
    for copy in copies:
        copy.start()
    for copy in copies:
        copy.wait()


def local(amplitudes, previous, coupling, thresholds, barrier, block_order, window_offset):
    points, rows, width = amplitudes.shape
    half = points // 2
    columns = coupling.shape[2]
    pieces = half * SPLIT
    bf16, f32 = jnp.bfloat16, jnp.float32
    sem = pltpu.SemaphoreType.DMA
    any_spec = pl.BlockSpec(memory_space=pl.ANY)
    vmem_spec = pl.BlockSpec(memory_space=pltpu.VMEM)
    staged = pl.pallas_call(
        kernel,
        out_shape=pltpu.VMEM((points, rows, width), bf16),
        in_specs=[any_spec] * 7,
        out_specs=vmem_spec,
        scratch_shapes=[
            pltpu.VMEM((points, columns // CHB, rows, CHB), bf16),
            pltpu.VMEM((4, points, rows, width), bf16),
            pltpu.VMEM((half, rows, width), bf16),
            pltpu.VMEM((half, rows, width), bf16),
            pltpu.VMEM((half, rows, width), bf16),
            pltpu.VMEM((half, rows, width), bf16),
            pltpu.VMEM((points, rows, width), bf16),
            pltpu.VMEM((points, rows, width), f32),
            pltpu.VMEM((rows, LANES), f32),
            pltpu.VMEM((rows, LANES), f32),
            pltpu.VMEM((points, TILE, LANES), f32),
            pltpu.SMEM((columns // CHB,), jnp.int32),
            pltpu.VMEM(thresholds.shape, f32),
            pltpu.VMEM(barrier.shape, f32),
            pltpu.SMEM(block_order.shape, jnp.int32),
            pltpu.SMEM(window_offset.shape, jnp.int32),
            sem((4,)),
            sem((points, columns // CHB)), sem, sem,
            sem, sem((pieces,)), sem, sem((pieces,)),
            sem, sem, sem((2 * pieces,)),
            sem, sem((points,)), sem, sem((2 * pieces,)),
            sem, sem, sem, sem,
        ],
        compiler_params=pltpu.CompilerParams(
            collective_id=0, has_side_effects=True, vmem_limit_bytes=60 << 20
        ),
        cost_estimate=pl.CostEstimate(
            flops=2 * points * rows * columns * width,
            bytes_accessed=2 * points * rows * (columns + 3 * width),
            transcendentals=0,
        ),
    )(amplitudes, previous, coupling, thresholds, barrier, block_order, window_offset)
    return pl.pallas_call(
        write_out,
        out_shape=jax.ShapeDtypeStruct((points, rows, width), bf16),
        in_specs=[vmem_spec],
        out_specs=any_spec,
        scratch_shapes=[sem((points,))],
        compiler_params=pltpu.CompilerParams(vmem_limit_bytes=40 << 20),
    )(staged)


def solution(mesh):
    placed = (
        P("radial", "chan", None),
        P("radial", "chan", None),
        P("radial", "chan", None),
        P("chan"),
        P("chan"),
        P(),
        P(),
    )
    return jax.shard_map(
        local, mesh=mesh, in_specs=placed, out_specs=P("radial", "chan", None), check_vma=False
    )
```

```python
import functools

import jax
import jax.numpy as jnp
from jax import lax
from jax.experimental import pallas as pl
from jax.experimental.pallas import tpu as pltpu
from jax.sharding import PartitionSpec as P

CHB = 128
GRID = 8192
SPLIT = 2
MESH = pl.DeviceIdType.MESH
TAPS = (-205.0 / 72, 8.0 / 5, -1.0 / 5, 8.0 / 315, -1.0 / 560)
LANES = 128
TILE = 16


def kernel(
    amp, prev, coup, thr_in, bar_in, order_in, offset_in, out,
    cbuf, vecs, relay_t, relay_a, halo_lo, halo_hi, pbuf, acc, thr_b, bar_b, scale, columns,
    thr, bar, order, offset, small_sem,
    coup_sem, own_sem, prev_sem,
    t_send, t_recv, a_send, a_recv, ft_send, fa_send, far_recv,
    sib_send, sib_recv, fs_send, fs_recv, up_send, up_recv, down_send, down_recv,
):
    points, rows, width = amp.shape
    half = points // 2
    per = rows // CHB
    radial, chan = lax.axis_index("radial"), lax.axis_index("chan")
    x, yl, z = lax.rem(radial, 4), lax.rem(lax.div(radial, 4), 2), lax.div(radial, 8)
    yh, core = lax.div(chan, 2), lax.rem(chan, 2)
    last = 3
    pieces = half * SPLIT
    size = rows // SPLIT
    far = vecs.at[2]

    def at(px, pyl, pz, pyh, pcore):
        return ((pz * 2 + pyl) * 4 + px, pyh * 2 + pcore)

    toward = at(x, 1 - yl, z, yh, core)
    away = at(x, 1 - yl, z, 1 - yh, core)
    sibling = at(x, yl, z, yh, 1 - core)
    up_z = jnp.where(x == last, z + (1 - yl), z)
    up_to = at(lax.rem(x + 1, 4), yl, jnp.minimum(up_z, 3), yh, core)
    has_up_to = up_z <= 3
    down_z = jnp.where(x == 0, z - yl, z)
    down_to = at(lax.rem(x + 3, 4), yl, jnp.maximum(down_z, 0), yh, core)
    has_down_to = down_z >= 0
    up_fz = jnp.where(x == 0, z - (1 - yl), z)
    up_from = at(lax.rem(x + 3, 4), yl, jnp.maximum(up_fz, 0), yh, core)
    has_up_from = up_fz >= 0
    down_fz = jnp.where(x == last, z + yl, z)
    down_from = at(lax.rem(x + 1, 4), yl, jnp.minimum(down_fz, 3), yh, core)
    has_down_from = down_fz <= 3
    t_base = jnp.where(x < 2, 0, half)
    a_base = half - t_base

    def remote(src, dst, send, recv, to):
        return pltpu.make_async_remote_copy(
            src_ref=src, dst_ref=dst, send_sem=send, recv_sem=recv, device_id=to, device_id_type=MESH
        )

    def piece(ref, first, i):
        row = pl.multiple_of((i % SPLIT) * size, size)
        return ref.at[first + i // SPLIT, pl.ds(row, size)]

    def own_t(i):
        return remote(
            piece(amp, t_base, i), piece(relay_t, 0, i), t_send, t_recv.at[i], toward
        )

    def own_a(i):
        return remote(
            piece(amp, a_base, i), piece(relay_a, 0, i), a_send, a_recv.at[i], away
        )

    def fwd_t(i):
        landed = far_recv.at[t_base * SPLIT + i]
        return remote(piece(relay_t, 0, i), piece(far, t_base, i), ft_send, landed, away)

    def fwd_a(i):
        landed = far_recv.at[a_base * SPLIT + i]
        return remote(piece(relay_a, 0, i), piece(far, a_base, i), fa_send, landed, toward)

    def own_sib(p):
        return remote(amp.at[p], vecs.at[1, p], sib_send, sib_recv.at[p], sibling)

    def fwd_sib(q):
        return remote(
            piece(far, 0, q), piece(vecs.at[3], 0, q), fs_send, fs_recv.at[q], sibling
        )

    def up_own(i):
        return remote(amp.at[half + i], halo_lo.at[i], up_send, up_recv, up_to)

    def up_relay(i):
        return remote(relay_t.at[i], halo_lo.at[i], up_send, up_recv, up_to)

    def down_own(i):
        return remote(amp.at[i], halo_hi.at[i], down_send, down_recv, down_to)

    def down_relay(i):
        return remote(relay_t.at[i], halo_hi.at[i], down_send, down_recv, down_to)

    blocks = coup.shape[2] // CHB

    def coup_copy(p, b):
        part = coup.at[p, :, b * CHB : (b + 1) * CHB]
        return pltpu.make_async_copy(part, cbuf.at[p, b], coup_sem.at[p, b])

    def coup_all(step):
        def one(p, _):
            for b in range(blocks):
                step(coup_copy(p, b))
            return 0

        lax.fori_loop(0, points, one, 0)

    small = [
        pltpu.make_async_copy(a, b, small_sem.at[i])
        for i, (a, b) in enumerate(
            ((thr_in, thr), (bar_in, bar), (order_in, order), (offset_in, offset))
        )
    ]
    own_copy = pltpu.make_async_copy(amp, vecs.at[0], own_sem)
    prev_copy = pltpu.make_async_copy(prev, pbuf, prev_sem)

    barrier = pltpu.get_barrier_semaphore()
    @pl.when(has_up_from)
    def _():
        pl.semaphore_signal(barrier, inc=1, device_id=up_from, device_id_type=MESH)

    @pl.when(has_down_from)
    def _():
        pl.semaphore_signal(barrier, inc=1, device_id=down_from, device_id_type=MESH)

    for to in (toward, away, sibling):
        pl.semaphore_signal(barrier, inc=1, device_id=to, device_id_type=MESH)

    own_copy.start()
    for copy in small:
        copy.start()
    pl.semaphore_wait(
        barrier, 3 + jnp.where(has_up_to, 1, 0) + jnp.where(has_down_to, 1, 0)
    )

    def send_own(i, _):
        own_t(i).start()
        own_a(i).start()
        return 0

    for i in range(pieces):
        send_own(i, 0)
    for p in range(points):
        own_sib(p).start()
    for i in range(half):
        @pl.when(x < last)
        def _(i=i):
            up_own(i).start()

        @pl.when(x > 0)
        def _(i=i):
            down_own(i).start()
    coup_all(lambda c: c.start())
    prev_copy.start()

    @pl.when(jnp.logical_not(has_up_from))
    def _():
        halo_lo[...] = jnp.zeros_like(halo_lo)

    @pl.when(jnp.logical_not(has_down_from))
    def _():
        halo_hi[...] = jnp.zeros_like(halo_hi)

    for copy in small:
        copy.wait()
    for j in range(per):
        part = slice(j * CHB, (j + 1) * CHB)
        thr_b[part, :] = jnp.broadcast_to(thr[part].reshape(1, CHB), (CHB, LANES)).T
        bar_b[part, :] = jnp.broadcast_to(bar[part].reshape(1, CHB), (CHB, LANES)).T
    for p in range(points):
        place = jnp.full((TILE, LANES), offset[0] + radial * points + p + 1, jnp.int32)
        s = place.astype(jnp.float32) * (1.0 / (GRID // 16))
        scale[p] = 1.0 / (1.0 + s * s)

    own_copy.wait()
    coup_all(lambda c: c.wait())

    sources = (chan, yh * 2 + 1 - core, (1 - yh) * 2 + core, (1 - yh) * 2 + 1 - core)

    def column(j):
        found = jnp.int32(0)
        for b in range(order.shape[0]):
            found = found + b * (1 - jnp.minimum((order[b] - j) * (order[b] - j), 1))
        return jnp.minimum(found, order.shape[0] - 1)

    for k, s in enumerate(sources):
        for j in range(per):
            columns[k * per + j] = column(s * per + j)

    def product(p, which, first=0, end=per):
        lhs = jnp.concatenate(
            [cbuf[p, columns[s * per + j]] for s in which for j in range(first, end)], axis=1
        )
        part = slice(first * CHB, end * CHB)
        rhs = jnp.concatenate([vecs[s, p, part, :] for s in which], axis=0)
        return jnp.dot(lhs, rhs, preferred_element_type=jnp.float32)

    def near_product(p, _):
        own_sib(p).wait_recv()
        acc[p] = product(p, (0, 1))
        return 0

    def first_hop(g, _):
        def pass_on(j, _):
            i = g * SPLIT + j
            own_t(i).wait_recv()
            fwd_t(i).start()
            own_a(i).wait_recv()
            fwd_a(i).start()
            return 0

        lax.fori_loop(0, SPLIT, pass_on, 0)

        @pl.when(jnp.logical_and(x == last, has_up_to))
        def _():
            up_relay(g).start()

        @pl.when(jnp.logical_and(x == 0, has_down_to))
        def _():
            down_relay(g).start()

        return 0

    lax.fori_loop(0, points, near_product, 0)
    lax.fori_loop(0, half, first_hop, 0)

    def arrive(i):
        def one(j, _):
            for base in (t_base, a_base):
                q = (base + i) * SPLIT + j
                here = piece(far, 0, q)
                remote(here, here, ft_send, far_recv.at[q], away).wait_recv()
                fwd_sib(q).start()
            return 0

        lax.fori_loop(0, SPLIT, one, 0)

    def passed(p, first, end):
        for j in range(first, end):
            fwd_sib(p * SPLIT + j).wait_recv()

    def finish(i):
        def one(h, _):
            p = i + h * half
            passed(p, 0, SPLIT)
            acc[p] += product(p, (2, 3))
            return 0

        lax.fori_loop(0, 2, one, 0)

    def finish_last(i):
        early = per - per // SPLIT

        def far_part(h, _):
            p = i + h * half
            acc[p] += product(p, (2,))
            return 0

        def near_part(h, _):
            p = i + h * half
            passed(p, 0, SPLIT - 1)
            acc[p] += product(p, (3,), 0, early)
            return 0

        def end_part(h, _):
            p = i + h * half
            passed(p, SPLIT - 1, SPLIT)
            total = acc[p] + product(p, (3,), early, per)
            out[p] = (total * (1.0 / 3.0)).astype(out.dtype)
            return 0

        lax.fori_loop(0, 2, far_part, 0)
        far_half = far.at[pl.ds(0, half)]
        remote(relay_t, far_half, ft_send, far_recv.at[0], away).wait_send()
        remote(relay_a, far_half, fa_send, far_recv.at[0], toward).wait_send()
        lax.fori_loop(0, 2, near_part, 0)
        lax.fori_loop(0, 2, end_part, 0)

    def store(i):
        for p in (i, i + half):
            out[p] = (acc[p] * (1.0 / 3.0)).astype(out.dtype)

    arrive(0)
    finish(0)
    arrive(1)
    finish(1)

    first_half = amp.at[pl.ds(0, half)]

    @pl.when(has_up_from)
    def _():
        remote(first_half, halo_lo, up_send, up_recv, up_to).wait_recv()

    @pl.when(has_down_from)
    def _():
        remote(first_half, halo_hi, down_send, down_recv, down_to).wait_recv()

    remote(amp, vecs.at[1], sib_send, sib_recv.at[0], sibling).wait_send()
    remote(first_half, relay_t, t_send, t_recv.at[0], toward).wait_send()
    remote(first_half, relay_a, a_send, a_recv.at[0], away).wait_send()

    @pl.when(has_up_to)
    def _():
        remote(first_half, halo_lo, up_send, up_recv, up_to).wait_send()

    @pl.when(has_down_to)
    def _():
        remote(first_half, halo_hi, down_send, down_recv, down_to).wait_send()

    prev_copy.wait()

    def stencil(r, _):
        tile = pl.ds(pl.multiple_of(r * TILE, TILE), TILE)
        for l in range(width // LANES):
            lane = slice(l * LANES, (l + 1) * LANES)
            v = [halo_lo[i, tile, lane].astype(jnp.float32) for i in range(half)]
            v += [vecs[0, i, tile, lane].astype(jnp.float32) for i in range(points)]
            v += [halo_hi[i, tile, lane].astype(jnp.float32) for i in range(half)]
            base = thr_b[tile, :] - (1.0 + 0.5 * TAPS[0])
            slope = bar_b[tile, :]
            for p in range(points):
                c = p + half
                total = (base + slope * scale[p]) * v[c]
                for m in range(1, 5):
                    total = total + (-0.5 * TAPS[m]) * (v[c - m] + v[c + m])
                total = total - 3.0 * pbuf[p, tile, lane].astype(jnp.float32)
                acc[p, tile, lane] = acc[p, tile, lane] + total
        return 0

    lax.fori_loop(0, rows // TILE, stencil, 0)
    store(0)
    store(1)
    arrive(2)
    finish(2)
    store(2)
    arrive(3)
    finish_last(3)

    remote(far, vecs.at[3], fs_send, fs_recv.at[0], sibling).wait_send()


def local(amplitudes, previous, coupling, thresholds, barrier, block_order, window_offset):
    points, rows, width = amplitudes.shape
    half = points // 2
    columns = coupling.shape[2]
    pieces = half * SPLIT
    bf16, f32 = jnp.bfloat16, jnp.float32
    sem = pltpu.SemaphoreType.DMA
    any_spec = pl.BlockSpec(memory_space=pl.ANY)
    vmem_spec = pl.BlockSpec(memory_space=pltpu.VMEM)
    staged = pl.pallas_call(
        kernel,
        out_shape=pltpu.VMEM((points, rows, width), bf16),
        in_specs=[any_spec] * 7,
        out_specs=vmem_spec,
        scratch_shapes=[
            pltpu.VMEM((points, columns // CHB, rows, CHB), bf16),
            pltpu.VMEM((4, points, rows, width), bf16),
            pltpu.VMEM((half, rows, width), bf16),
            pltpu.VMEM((half, rows, width), bf16),
            pltpu.VMEM((half, rows, width), bf16),
            pltpu.VMEM((half, rows, width), bf16),
            pltpu.VMEM((points, rows, width), bf16),
            pltpu.VMEM((points, rows, width), f32),
            pltpu.VMEM((rows, LANES), f32),
            pltpu.VMEM((rows, LANES), f32),
            pltpu.VMEM((points, TILE, LANES), f32),
            pltpu.SMEM((columns // CHB,), jnp.int32),
            pltpu.VMEM(thresholds.shape, f32),
            pltpu.VMEM(barrier.shape, f32),
            pltpu.SMEM(block_order.shape, jnp.int32),
            pltpu.SMEM(window_offset.shape, jnp.int32),
            sem((4,)),
            sem((points, columns // CHB)), sem, sem,
            sem, sem((pieces,)), sem, sem((pieces,)),
            sem, sem, sem((2 * pieces,)),
            sem, sem((points,)), sem, sem((2 * pieces,)),
            sem, sem, sem, sem,
        ],
        compiler_params=pltpu.CompilerParams(
            collective_id=0, has_side_effects=True, vmem_limit_bytes=60 << 20
        ),
        cost_estimate=pl.CostEstimate(
            flops=2 * points * rows * columns * width,
            bytes_accessed=2 * points * rows * (columns + 3 * width),
            transcendentals=0,
        ),
    )(amplitudes, previous, coupling, thresholds, barrier, block_order, window_offset)
    return staged


def solution(mesh):
    placed = (
        P("radial", "chan", None),
        P("radial", "chan", None),
        P("radial", "chan", None),
        P("chan"),
        P("chan"),
        P(),
        P(),
    )
    return jax.shard_map(
        local, mesh=mesh, in_specs=placed, out_specs=P("radial", "chan", None), check_vma=False
    )
```
